32 devices in a mesh: gx: 4 (over y, core), gy: 8 (over z, x).
Axes of the slice: x: 2, y: 2, z: 4, core: 2. Of those that a mesh axis runs over, the one named last changes fastest.
Arguments:
- state: float32 [286, 2, 16, 512], P(None, None, 'gy', 'gx'), may hold values from -6 to 6
- adjoint: float32 [286, 2, 16, 512], P(None, None, 'gy', 'gx'), may hold values from -6 to 6
- upwind_pos: float32 [3, 286, 286], replicated, may hold values from -0.375 to 0.375
- upwind_neg: float32 [3, 286, 286], replicated, may hold values from -0.375 to 0.375
- collision: float32 [35, 35, 35], replicated, may hold values from -0.15625 to 0.15625
- relax: float32 [286], replicated, may hold values from 0.1 to 2
- wall_table: float32 [3, 286], replicated, may hold values from 0 to 2
- drag_weights: float32 [286], replicated, may hold values from -6 to 6
- block_inverse: float32 [286, 286], replicated, may hold values from -0.375 to 0.375
- cell_codes: int32 [2, 16, 512], P(None, 'gy', 'gx'), may hold values from 0 to 3
- wall_mask: int32 [2, 16, 512], P(None, 'gy', 'gx'), may hold values 0 or 1
Outputs:
- state_next: float32 [286, 2, 16, 512], P(None, None, 'gy', 'gx')
- adjoint_next: float32 [286, 2, 16, 512], P(None, None, 'gy', 'gx')
The draws below stay inside these ranges and needn't reach their ends.
All inputs are finite; a program needn't handle non-finite values. No bound on the sum of `wall_mask` on one device may be relied on, other than what follows from the above.
Results may differ from the reference program's by a relative error of at most 0.0003.
Values sent between devices are 32-bit elements; how exact they have to be, the bound alone decides.
A program may use at most 64 MiB of HBM per device.

```python
import math
import jax
import jax.numpy as jnp
from jax import lax

M = 286
MLOW = 35
PLANES = 2
NX = 512
NY = 16


def place_ends(result, key, least, top_value):
    longest = result.shape.index(max(result.shape))
    spots = []
    for shift in (0, 1):
        where = [jax.random.randint(jax.random.fold_in(key, axis), (), 0, length) for axis, length in enumerate(result.shape)]
        where[longest] = (where[longest] + shift) % result.shape[longest]
        spots.append(tuple(where))
    return result.at[spots[0]].set(least).at[spots[1]].set(top_value)


def block_scale(rng, extent, pieces, low, largest):
    loudness, own = 1.0, jax.random.fold_in(rng, 6)
    for axis_at, blocks in pieces:
        draws = jnp.exp(jax.random.uniform(jax.random.fold_in(own, axis_at), (blocks,), jnp.float32, low / len(pieces), largest / len(pieces)))
        loudness = loudness * jnp.repeat(draws, extent[axis_at] // blocks).reshape([-1 if axis == axis_at else 1 for axis in range(len(extent))])
    return loudness


def normal_values(rng, extent, spread, most, shards=(), kind=jnp.bfloat16):
    drawn = spread * jax.random.normal(rng, extent, jnp.float32)
    if shards:
        drawn = drawn * block_scale(rng, extent, shards, -0.22, 0.18)
    return jnp.clip(drawn, -most, most).astype(kind)


def setup_inputs(seed: int = 0) -> dict:
    streams_of = jax.random.split(jax.random.key(seed), 12)
    return {
        "state": normal_values(streams_of[0], (M, PLANES, NY, NX), 1.0, 6.0, ((2, 8), (3, 4)), jnp.float32),
        "adjoint": normal_values(streams_of[1], (M, PLANES, NY, NX), 1.0, 6.0, ((2, 8), (3, 4)), jnp.float32),
        "upwind_pos": normal_values(streams_of[2], (3, M, M), M ** -0.5, 0.375, (), jnp.float32),
        "upwind_neg": normal_values(streams_of[3], (3, M, M), M ** -0.5, 0.375, (), jnp.float32),
        "collision": normal_values(streams_of[4], (MLOW, MLOW, MLOW), (MLOW * MLOW) ** -0.5, 0.15625, (), jnp.float32),
        "relax": jnp.clip(jnp.exp(jax.random.uniform(streams_of[5], (M,), jnp.float32, math.log(0.1), math.log(2.0))), 0.1, 2.0),
        "wall_table": jnp.clip(jax.random.uniform(streams_of[6], (3, M), jnp.float32, 0.0, 2.0), 0.0, 2.0),
        "drag_weights": normal_values(streams_of[7], (M,), 1.0, 6.0, (), jnp.float32),
        "block_inverse": normal_values(streams_of[8], (M, M), M ** -0.5, 0.375, (), jnp.float32),
        "cell_codes": place_ends(jax.random.randint(streams_of[9], (PLANES, NY, NX), 0, 4), jax.random.fold_in(streams_of[9], 1), 0, 3).astype(jnp.int32),
        "wall_mask": place_ends((jax.random.randint(streams_of[10], (PLANES, NY, NX), 0, 4) < 1).astype(jnp.int32), jax.random.fold_in(streams_of[10], 1), 0, 1),
    }


def apply_matrix(matrix, field):
    return jnp.dot(matrix, field, precision=lax.Precision.HIGHEST)


def reference(state, adjoint, upwind_pos, upwind_neg, collision, relax, wall_table, drag_weights, block_inverse, cell_codes, wall_mask):
    moments = state.shape[0]
    depth = state.shape[1]
    height = state.shape[2]
    width = state.shape[3]
    lowest = collision.shape[0]
    flat_gain = collision.reshape(lowest, lowest * lowest)
    symmetric = collision + jnp.transpose(collision, (0, 2, 1))
    flat_adgain = jnp.transpose(symmetric, (1, 0, 2)).reshape(lowest, lowest * lowest)

    def take_row(field, zpos, ypos):
        valid = jnp.logical_and(ypos >= 0, ypos < height)
        yclip = jnp.clip(ypos, 0, height - 1).astype(jnp.int32)
        start = (jnp.int32(0), zpos.astype(jnp.int32), yclip, jnp.int32(0))
        row = lax.dynamic_slice(field, start, (moments, 1, 1, width)).reshape(moments, width)
        return jnp.where(valid, row, jnp.zeros_like(row))

    def one_row(index):
        zplane = index // height
        yrow = index % height
        zlow = (zplane + depth - 1) % depth
        zhigh = (zplane + 1) % depth
        results = []
        for field, is_adjoint in ((state, False), (adjoint, True)):
            center = take_row(field, zplane, yrow)
            xminus = jnp.pad(center, ((0, 0), (1, 0)))[:, :-1]
            xplus = jnp.pad(center, ((0, 0), (0, 1)))[:, 1:]
            yminus = take_row(field, zplane, yrow - 1)
            yplus = take_row(field, zplane, yrow + 1)
            zminus = take_row(field, zlow, yrow)
            zplus = take_row(field, zhigh, yrow)
            minus_all = (xminus, yminus, zminus)
            plus_all = (xplus, yplus, zplus)
            total = jnp.zeros_like(center)
            for direction in range(3):
                if is_adjoint:
                    total = total + apply_matrix(upwind_pos[direction].T, center - plus_all[direction])
                    total = total + apply_matrix(upwind_neg[direction].T, minus_all[direction] - center)
                else:
                    total = total + apply_matrix(upwind_pos[direction], center - minus_all[direction])
                    total = total + apply_matrix(upwind_neg[direction], plus_all[direction] - center)
            results.append((center, total))
        (state_row, stream), (adjoint_row, adstream) = results
        codes = lax.dynamic_slice(cell_codes, (zplane.astype(jnp.int32), yrow.astype(jnp.int32), jnp.int32(0)), (1, 1, width)).reshape(width)
        walls = lax.dynamic_slice(wall_mask, (zplane.astype(jnp.int32), yrow.astype(jnp.int32), jnp.int32(0)), (1, 1, width)).reshape(width)
        onehot = (codes[None, :] == jnp.arange(1, 4, dtype=jnp.int32)[:, None]).astype(state.dtype)
        damp = relax[:, None] + apply_matrix(wall_table.T, onehot)
        state_low = state_row[:lowest]
        adjoint_low = adjoint_row[:lowest]
        products = (state_low[:, None, :] * state_low[None, :, :]).reshape(lowest * lowest, width)
        gain = jnp.pad(apply_matrix(flat_gain, products), ((0, moments - lowest), (0, 0)))
        cross = (adjoint_low[:, None, :] * state_low[None, :, :]).reshape(lowest * lowest, width)
        adgain = jnp.pad(apply_matrix(flat_adgain, cross), ((0, moments - lowest), (0, 0)))
        primal_res = stream - gain + damp * state_row
        state_new = state_row - 0.5 * apply_matrix(block_inverse, primal_res)
        adjoint_res = adstream - adgain + damp * adjoint_row - walls.astype(state.dtype)[None, :] * drag_weights[:, None]
        adjoint_new = adjoint_row - 0.5 * apply_matrix(block_inverse.T, adjoint_res)
        return state_new, adjoint_new

    rows_state, rows_adjoint = lax.map(one_row, jnp.arange(depth * height, dtype=jnp.int32))
    state_next = jnp.transpose(rows_state.reshape(depth, height, moments, width), (2, 0, 1, 3))
    adjoint_next = jnp.transpose(rows_adjoint.reshape(depth, height, moments, width), (2, 0, 1, 3))
    return state_next, adjoint_next
```

```python
import functools
import jax
import jax.numpy as jnp
from jax import lax
from jax.experimental import pallas as pl
from jax.experimental.pallas import tpu as pltpu
from jax.sharding import PartitionSpec as P

F32 = jnp.float32
BF16 = jnp.bfloat16
MESH = pl.DeviceIdType.MESH

PX, NX, PY, NY, DZ, BI, HALO_PREV, HALO_NEXT = range(8)
N_SLOTS = 8


def split(x):
    high = x.astype(BF16)
    return high, (x - high.astype(F32)).astype(BF16)


def dot3(a_high, a_low, b_high, b_low):
    def dot(a, b):
        return jnp.dot(a, b, preferred_element_type=F32)

    return dot(a_high, b_high) + (dot(a_high, b_low) + dot(a_low, b_high))


def kernel(
    sizes,
    state, adjoint, pos, neg, coll, relax, table, drag, inverse, codes, walls,
    state_out, adjoint_out,
    lin, pos_v, neg_v, coll_v, relax_v, table_v, drag_v, inv_v, codes_v, walls_v,
    field, xsend, xrecv, halo, w_high, w_low, sym, zed, low, res, vecs, out_lin,
    in_sem, out_sem, xs_sem, xr_sem, ys_sem, yr_sem,
):
    moments, planes, rows, width, lowest, low_pad, n_gx, n_gy = sizes
    cells = planes * rows
    gx, gy = lax.axis_index("gx"), lax.axis_index("gy")
    has = {
        ("gx", 0): gx > 0, ("gx", 1): gx < n_gx - 1,
        ("gy", 0): gy > 0, ("gy", 1): gy < n_gy - 1,
    }
    where = {("gx", 0): gx - 1, ("gx", 1): gx + 1, ("gy", 0): gy - 1, ("gy", 1): gy + 1}

    loads = [
        pltpu.make_async_copy(src, dst, in_sem.at[i])
        for i, (src, dst) in enumerate(
            (
                (state, lin.at[0]), (adjoint, lin.at[1]), (coll, coll_v), (pos, pos_v),
                (neg, neg_v), (inverse, inv_v), (relax, relax_v), (table, table_v),
                (drag, drag_v), (codes, codes_v), (walls, walls_v),
            )
        )
    ]
    for load in loads:
        load.start()

    barrier = pltpu.get_barrier_semaphore()
    for side, there in has.items():
        @pl.when(there)
        def _(side=side):
            pl.semaphore_signal(
                barrier, inc=1, device_id={side[0]: where[side]}, device_id_type=MESH
            )
    pl.semaphore_wait(barrier, sum(there.astype(jnp.int32) for there in has.values()))

    def y_copy(f, to):
        return pltpu.make_async_remote_copy(
            src_ref=field.at[f, (rows - 1) * to],
            dst_ref=halo.at[f, 1 - to],
            send_sem=ys_sem.at[f, to],
            recv_sem=yr_sem.at[f, 1 - to],
            device_id={"gy": where["gy", to]},
            device_id_type=MESH,
        )

    def x_copy(to):
        return pltpu.make_async_remote_copy(
            src_ref=xsend.at[to],
            dst_ref=xrecv.at[1 - to],
            send_sem=xs_sem.at[to],
            recv_sem=xr_sem.at[1 - to],
            device_id={"gx": where["gx", to]},
            device_id_type=MESH,
        )

    for f in range(2):
        loads[f].wait()
        for p in range(planes):
            for y in range(rows):
                field[f, y, :, p * width:(p + 1) * width] = lin[
                    f, pl.ds(p * rows + y, moments, stride=cells), :
                ]
        for to in range(2):
            @pl.when(has["gy", to])
            def _(f=f, to=to):
                y_copy(f, to).start()

    lanes = lax.broadcasted_iota(jnp.int32, (moments, width), 1)
    firsts = jnp.zeros((moments, width), F32)
    lasts = jnp.zeros((moments, width), F32)
    for f in range(2):
        for p in range(planes):
            for y in range(rows):
                spot = f * cells + p * rows + y
                block = field[f, y, :, p * width:(p + 1) * width]
                firsts = jnp.where(lanes == spot, pltpu.roll(block, spot, 1), firsts)
                lasts = jnp.where(lanes == spot, pltpu.roll(block, spot + 1, 1), lasts)
    xsend[0] = firsts
    xsend[1] = lasts
    for to in range(2):
        @pl.when(has["gx", to])
        def _(to=to):
            x_copy(to).start()

        @pl.when(jnp.logical_not(has["gx", to]))
        def _(to=to):
            xrecv[to] = jnp.zeros((moments, width), F32)

        @pl.when(jnp.logical_not(has["gy", to]))
        def _(to=to):
            for f in range(2):
                halo[f, to] = jnp.zeros((moments, planes * width), F32)

    loads[2].wait()
    sym[...] = jnp.zeros(sym.shape, F32)
    for k in range(lowest):
        c = coll_v[k]
        sym[k * low_pad:k * low_pad + lowest, :] = 0.5 * (c + c.T)
    sym_high, sym_low = split(sym[...])
    for y in range(rows):
        s_low = field[0, y, :lowest, :]
        a_low = field[1, y, :lowest, :]
        zed[...] = dot3(sym_high, sym_low, *split(s_low))
        adgain = jnp.zeros(a_low.shape, F32)
        for k in range(lowest):
            z_k = zed[k * low_pad:k * low_pad + lowest, :]
            low[0, y, k:k + 1, :] = jnp.sum(z_k * s_low, axis=0, keepdims=True)
            adgain = adgain + z_k * a_low[k:k + 1, :]
        low[1, y, :lowest, :] = 2.0 * adgain

    for load in loads[3:]:
        load.wait()

    def keep(f, slot, matrix):
        high, rest = split(matrix)
        w_high[f, slot] = high
        w_low[f, slot] = rest

    for slot, matrix in (
        (PX, pos_v[0]), (NX, neg_v[0]), (PY, pos_v[1]), (NY, neg_v[1]),
        (DZ, pos_v[2] - neg_v[2]), (BI, inv_v[...]),
    ):
        keep(0, slot, matrix)
        keep(1, slot, matrix.T)

    def times(f, slot, x):
        return dot3(w_high[f, slot], w_low[f, slot], *split(x))

    def product(f, slot, scale):
        return scale * dot3(w_high[f, BI], w_low[f, BI], w_high[f, slot], w_low[f, slot])

    keep(0, HALO_PREV, product(0, PY, 0.5))
    keep(0, HALO_NEXT, product(0, NY, -0.5))
    keep(1, HALO_PREV, product(1, NY, -0.5))
    keep(1, HALO_NEXT, product(1, PY, 0.5))

    vecs[...] = jnp.zeros(vecs.shape, F32)
    vecs[0:3, :] = table_v[...]
    vecs[3:4, :] = relax_v[...].reshape(1, moments)
    vecs[4:5, :] = drag_v[...].reshape(1, moments)

    for to in range(2):
        @pl.when(has["gx", to])
        def _(to=to):
            x_copy(1 - to).wait_recv()

    edge = lax.broadcasted_iota(jnp.int32, (moments, width), 1)
    kinds = lax.broadcasted_iota(jnp.int32, (8, width), 0)

    def spread(table):
        return lax.dot_general(
            vecs[...], table, (((0,), (0,)), ((), ())),
            precision=lax.Precision.HIGHEST, preferred_element_type=F32,
        )

    for f in range(2):
        back, ahead = (PX, NX) if f == 0 else (NX, PX)
        y_back, y_ahead = (PY, NY) if f == 0 else (NY, PY)
        sign = 1.0 if f == 0 else -1.0
        z_diff = [field[f, y, :, :width] - field[f, y, :, width:] for y in range(rows)]
        z_part = times(f, DZ, jnp.concatenate(z_diff, axis=1))
        for y in range(rows):
            here = field[f, y]
            minus, plus, ones, marks = [], [], [], []
            for p in range(planes):
                spot = f * cells + p * rows + y
                block = here[:, p * width:(p + 1) * width]
                minus.append(jnp.where(
                    edge == 0, xrecv[0, :, spot:spot + 1], pltpu.roll(block, 1, 1)))
                plus.append(jnp.where(
                    edge == width - 1, xrecv[1, :, spot:spot + 1],
                    pltpu.roll(block, width - 1, 1)))
                code = codes_v[p, y:y + 1, :]
                ones.append(jnp.where(
                    kinds < 3, (code == kinds + 1).astype(F32), (kinds == 3).astype(F32)))
                wall = walls_v[p, y:y + 1, :].astype(F32)
                marks.append(jnp.where(kinds == 4, wall, 0.0))
            minus = jnp.concatenate(minus, axis=1)
            plus = jnp.concatenate(plus, axis=1)
            total = sign * (times(f, back, here - minus) + times(f, ahead, plus - here))
            y_minus = here - field[f, y - 1] if y > 0 else here
            y_plus = field[f, y + 1] - here if y < rows - 1 else -here
            total = total + sign * (times(f, y_back, y_minus) + times(f, y_ahead, y_plus))
            z_here = z_part[:, y * width:(y + 1) * width]
            total = total + jnp.concatenate([z_here, -z_here], axis=1)
            total = total + spread(jnp.concatenate(ones, axis=1)) * here
            if f == 1:
                total = total - spread(jnp.concatenate(marks, axis=1))
            res[...] = total
            res[:lowest, :] = res[:lowest, :] - low[f, y, :lowest, :]
            zed_out = here - 0.5 * times(f, BI, res[...])
            for p in range(planes):
                out_lin[f, pl.ds(p * rows + y, moments, stride=cells), :] = zed_out[
                    :, p * width:(p + 1) * width
                ]

    stores = []
    for f, target in enumerate((state_out, adjoint_out)):
        for side, y, slot in ((0, 0, HALO_PREV), (1, rows - 1, HALO_NEXT)):
            @pl.when(has["gy", side])
            def _(f=f, side=side):
                y_copy(f, 1 - side).wait_recv()

            late = times(f, slot, halo[f, side])
            for p in range(planes):
                spots = pl.ds(p * rows + y, moments, stride=cells)
                out_lin[f, spots, :] = out_lin[f, spots, :] + late[:, p * width:(p + 1) * width]
        store = pltpu.make_async_copy(out_lin.at[f], target, out_sem.at[f])
        store.start()
        stores.append(store)

    for to in range(2):
        @pl.when(has["gx", to])
        def _(to=to):
            x_copy(to).wait_send()

        @pl.when(has["gy", to])
        def _(to=to):
            for f in range(2):
                y_copy(f, to).wait_send()
    for store in stores:
        store.wait()


def on_device(
    n_gx, n_gy, state, adjoint, upwind_pos, upwind_neg, collision, relax, wall_table,
    drag_weights, block_inverse, cell_codes, wall_mask,
):
    moments, planes, rows, width = state.shape
    lowest = collision.shape[0]
    assert planes == 2 and 2 * planes * rows <= width
    low_pad = -(-lowest // 8) * 8
    flat = (moments * planes * rows, width)
    sizes = (moments, planes, rows, width, lowest, low_pad, n_gx, n_gy)
    out = jax.ShapeDtypeStruct(flat, F32)
    anywhere = pl.BlockSpec(memory_space=pl.ANY)
    outs = pl.pallas_call(
        functools.partial(kernel, sizes),
        out_shape=(out, out),
        in_specs=[pl.BlockSpec(memory_space=pltpu.HBM)] * 11,
        out_specs=(anywhere, anywhere),
        scratch_shapes=[
            pltpu.VMEM((2,) + flat, F32),
            pltpu.VMEM(upwind_pos.shape, F32),
            pltpu.VMEM(upwind_neg.shape, F32),
            pltpu.VMEM(collision.shape, F32),
            pltpu.VMEM(relax.shape, F32),
            pltpu.VMEM(wall_table.shape, F32),
            pltpu.VMEM(drag_weights.shape, F32),
            pltpu.VMEM(block_inverse.shape, F32),
            pltpu.VMEM(cell_codes.shape, jnp.int32),
            pltpu.VMEM(wall_mask.shape, jnp.int32),
            pltpu.VMEM((2, rows, moments, planes * width), F32),
            pltpu.VMEM((2, moments, width), F32),
            pltpu.VMEM((2, moments, width), F32),
            pltpu.VMEM((2, 2, moments, planes * width), F32),
            pltpu.VMEM((2, N_SLOTS, moments, moments), BF16),
            pltpu.VMEM((2, N_SLOTS, moments, moments), BF16),
            pltpu.VMEM((lowest * low_pad, lowest), F32),
            pltpu.VMEM((lowest * low_pad, planes * width), F32),
            pltpu.VMEM((2, rows, low_pad, planes * width), F32),
            pltpu.VMEM((moments, planes * width), F32),
            pltpu.VMEM((8, moments), F32),
            pltpu.VMEM((2,) + flat, F32),
            pltpu.SemaphoreType.DMA((11,)),
            pltpu.SemaphoreType.DMA((2,)),
            pltpu.SemaphoreType.DMA((2,)),
            pltpu.SemaphoreType.DMA((2,)),
            pltpu.SemaphoreType.DMA((2, 2)),
            pltpu.SemaphoreType.DMA((2, 2)),
        ],
        compiler_params=pltpu.CompilerParams(
            collective_id=0, has_side_effects=True, vmem_limit_bytes=52 * 1024 * 1024
        ),
    )(
        state.reshape(flat), adjoint.reshape(flat), upwind_pos, upwind_neg, collision, relax,
        wall_table, drag_weights, block_inverse, cell_codes, wall_mask,
    )
    return tuple(o.reshape(state.shape) for o in outs)


def solution(mesh):
    in_specs = (
        P(None, None, "gy", "gx"),
        P(None, None, "gy", "gx"),
        P(),
        P(),
        P(),
        P(),
        P(),
        P(),
        P(),
        P(None, "gy", "gx"),
        P(None, "gy", "gx"),
    )
    out_specs = (P(None, None, "gy", "gx"), P(None, None, "gy", "gx"))
    return jax.shard_map(
        functools.partial(on_device, mesh.shape["gx"], mesh.shape["gy"]),
        mesh=mesh, in_specs=in_specs, out_specs=out_specs, check_vma=False,
    )
```

```python
import functools
import jax
import jax.numpy as jnp
from jax import lax
from jax.experimental import pallas as pl
from jax.experimental.pallas import tpu as pltpu
from jax.sharding import PartitionSpec as P

F32 = jnp.float32
BF16 = jnp.bfloat16
MESH = pl.DeviceIdType.MESH

PX, NX, PY, NY, DZ = range(5)
BLOCKS = 5
PIECES = 4
BI, HALO_PREV, HALO_NEXT = range(3)


def split(x):
    high = x.astype(BF16)
    return high, (x - high.astype(F32)).astype(BF16)


def dot(a, b):
    return jnp.dot(a, b, preferred_element_type=F32)


def dot3(a_high, a_low, b_high, b_low):
    return dot(a_high, b_high) + (dot(a_high, b_low) + dot(a_low, b_high))


def kernel(
    sizes,
    state, adjoint, pos, neg, coll, relax, table, drag, inverse, codes, walls,
    state_out, adjoint_out,
    lin, pos_v, neg_v, coll_v, relax_v, table_v, drag_v, inv_v, codes_v, walls_v,
    field, xsend, xrecv, halo, wide, wide_high, wide_low, tri, tri_b, rhs_high, rhs_low,
    sym, zed, low, res, vecs, out_lin,
    in_sem, out_sem, xs_sem, xr_sem, ys_sem, yr_sem,
):
    moments, planes, rows, width, lowest, low_pad, padded, n_gx, n_gy = sizes
    cells = planes * rows
    gx, gy = lax.axis_index("gx"), lax.axis_index("gy")
    has = {
        ("gx", 0): gx > 0, ("gx", 1): gx < n_gx - 1,
        ("gy", 0): gy > 0, ("gy", 1): gy < n_gy - 1,
    }
    where = {("gx", 0): gx - 1, ("gx", 1): gx + 1, ("gy", 0): gy - 1, ("gy", 1): gy + 1}

    loads = [
        pltpu.make_async_copy(src, dst, in_sem.at[i])
        for i, (src, dst) in enumerate(
            (
                (state, lin.at[0]), (adjoint, lin.at[1]), (coll, coll_v), (pos, pos_v),
                (neg, neg_v), (inverse, inv_v), (relax, relax_v), (table, table_v),
                (drag, drag_v), (codes, codes_v), (walls, walls_v),
            )
        )
    ]
    for load in loads:
        load.start()

    barrier = pltpu.get_barrier_semaphore()
    for side, there in has.items():
        @pl.when(there)
        def _(side=side):
            pl.semaphore_signal(
                barrier, inc=1, device_id={side[0]: where[side]}, device_id_type=MESH
            )
    field[:, :, moments:, :] = jnp.zeros((2, rows, padded - moments, planes * width), F32)
    pl.semaphore_wait(barrier, sum(there.astype(jnp.int32) for there in has.values()))

    def y_copy(f, to):
        return pltpu.make_async_remote_copy(
            src_ref=field.at[f, (rows - 1) * to],
            dst_ref=halo.at[f, 1 - to],
            send_sem=ys_sem.at[f, to],
            recv_sem=yr_sem.at[f, 1 - to],
            device_id={"gy": where["gy", to]},
            device_id_type=MESH,
        )

    def x_copy(to):
        return pltpu.make_async_remote_copy(
            src_ref=xsend.at[to],
            dst_ref=xrecv.at[1 - to],
            send_sem=xs_sem.at[to],
            recv_sem=xr_sem.at[1 - to],
            device_id={"gx": where["gx", to]},
            device_id_type=MESH,
        )

    for f in range(2):
        loads[f].wait()
        for p in range(planes):
            for y in range(rows):
                field[f, y, :moments, p * width:(p + 1) * width] = lin[
                    f, pl.ds(p * rows + y, moments, stride=cells), :
                ]
        for to in range(2):
            @pl.when(has["gy", to])
            def _(f=f, to=to):
                y_copy(f, to).start()

    lanes = lax.broadcasted_iota(jnp.int32, (padded, width), 1)
    firsts = jnp.zeros((padded, width), F32)
    lasts = jnp.zeros((padded, width), F32)
    for f in range(2):
        for p in range(planes):
            for y in range(rows):
                spot = f * cells + p * rows + y
                block = field[f, y, :, p * width:(p + 1) * width]
                firsts = jnp.where(lanes == spot, pltpu.roll(block, spot, 1), firsts)
                lasts = jnp.where(lanes == spot, pltpu.roll(block, spot + 1, 1), lasts)
    xsend[0] = firsts
    xsend[1] = lasts
    for to in range(2):
        @pl.when(has["gx", to])
        def _(to=to):
            x_copy(to).start()

        @pl.when(jnp.logical_not(has["gx", to]))
        def _(to=to):
            xrecv[to] = jnp.zeros((padded, width), F32)

        @pl.when(jnp.logical_not(has["gy", to]))
        def _(to=to):
            for f in range(2):
                halo[f, to] = jnp.zeros((padded, planes * width), F32)

    loads[2].wait()
    sym[...] = jnp.zeros(sym.shape, F32)
    for k in range(lowest):
        c = coll_v[k]
        sym[k * low_pad:k * low_pad + lowest, :lowest] = 0.5 * (c + c.T)
    half = sym.shape[1] // 2
    sym_all = sym[...]
    sym_top = sym_all.astype(BF16).astype(F32)
    sym_k = jnp.concatenate(
        [(sym_top + pltpu.roll(sym_top, half, 1)).astype(BF16), (sym_all - sym_top).astype(BF16)],
        axis=1,
    )
    for y in range(rows):
        s_low = field[0, y, :lowest, :]
        a_low = field[1, y, :lowest, :]
        s_pad = field[0, y, :half, :]
        keep_rows = lax.broadcasted_iota(jnp.int32, s_pad.shape, 0) < lowest
        s_high, s_rest = split(jnp.where(keep_rows, s_pad, 0.0))
        s_k = jnp.concatenate([s_high, s_rest, s_high, jnp.zeros_like(s_high)], axis=0)
        zed[...] = dot(sym_k, s_k)
        adgain = jnp.zeros(a_low.shape, F32)
        for k in range(lowest):
            z_k = zed[k * low_pad:k * low_pad + lowest, :]
            low[0, y, k:k + 1, :] = jnp.sum(z_k * s_low, axis=0, keepdims=True)
            adgain = adgain + z_k * a_low[k:k + 1, :]
        low[1, y, :lowest, :] = 2.0 * adgain

    for load in loads[3:]:
        load.wait()

    wide[...] = jnp.zeros(wide.shape, F32)
    tri[...] = jnp.zeros(tri.shape, F32)
    originals = (pos_v[0], neg_v[0], pos_v[1], neg_v[1], pos_v[2] - neg_v[2])

    def keep(f, slot, matrix):
        top = matrix.astype(BF16).astype(F32)
        tri[:moments, :moments] = top
        tri[:moments, padded:padded + moments] = top
        tri[:moments, 2 * padded:2 * padded + moments] = matrix - top
        tri_b[f, slot] = tri[...].astype(BF16)

    def times(f, slot, x):
        high, rest = split(x)
        return dot(tri_b[f, slot], jnp.concatenate([high, rest, high], axis=0))

    for f in range(2):
        for i, matrix in enumerate(originals):
            wide[:moments, i * padded:i * padded + moments] = matrix if f == 0 else matrix.T
        wide_high[f], wide_low[f] = split(wide[...])
        inv = inv_v[...] if f == 0 else inv_v[...].T
        inv_high, inv_low = split(inv)
        keep(f, BI, inv)
        for slot, block, scale in (
            (HALO_PREV, PY if f == 0 else NY, 0.5 if f == 0 else -0.5),
            (HALO_NEXT, NY if f == 0 else PY, -0.5 if f == 0 else 0.5),
        ):
            matrix = originals[block] if f == 0 else originals[block].T
            keep(f, slot, scale * dot3(inv_high, inv_low, *split(matrix)))

    vecs[...] = jnp.zeros(vecs.shape, F32)
    vecs[0:3, :moments] = table_v[...]
    vecs[3:4, :moments] = relax_v[...].reshape(1, moments)
    vecs[4:5, :moments] = drag_v[...].reshape(1, moments)
    whole = vecs[...]
    part1 = whole.astype(BF16).astype(F32)
    part2 = (whole - part1).astype(BF16).astype(F32)
    part3 = whole - part1 - part2
    parts = jnp.concatenate([part1, part2, part3], axis=0).T.astype(BF16)

    def spread(flags):
        return dot(parts, jnp.concatenate([flags] * 3, axis=0).astype(BF16))

    for to in range(2):
        @pl.when(has["gx", to])
        def _(to=to):
            x_copy(1 - to).wait_recv()

    kinds = lax.broadcasted_iota(jnp.int32, (8, width), 0)
    for y in range(rows):
        ones, marks = [], []
        for p in range(planes):
            code = codes_v[p, y:y + 1, :]
            ones.append(jnp.where(
                kinds < 3, (code == kinds + 1).astype(F32), (kinds == 3).astype(F32)))
            wall = walls_v[p, y:y + 1, :].astype(F32)
            marks.append(jnp.where(kinds == 4, wall, 0.0))
        damp = spread(jnp.concatenate(ones, axis=1))
        pull = spread(jnp.concatenate(marks, axis=1))
        for f in range(2):
            here = field[f, y]
            minus, plus = [], []
            for p in range(planes):
                spot = f * cells + p * rows + y
                block = here[:, p * width:(p + 1) * width]
                minus.append(jnp.where(
                    lanes == 0, xrecv[0, :, spot:spot + 1], pltpu.roll(block, 1, 1)))
                plus.append(jnp.where(
                    lanes == width - 1, xrecv[1, :, spot:spot + 1],
                    pltpu.roll(block, width - 1, 1)))
            x_minus = here - jnp.concatenate(minus, axis=1)
            x_plus = jnp.concatenate(plus, axis=1) - here
            y_minus = here - field[f, y - 1] if y > 0 else here
            y_plus = field[f, y + 1] - here if y < rows - 1 else -here
            z_diff = here[:, :width] - here[:, width:]
            z_both = jnp.concatenate([z_diff, -z_diff], axis=1)
            if f == 0:
                terms = (x_minus, x_plus, y_minus, y_plus, z_both)
            else:
                terms = (-x_plus, -x_minus, -y_plus, -y_minus, z_both)
            for i, term in enumerate(terms):
                rhs_high[i * padded:(i + 1) * padded, :], rhs_low[i * padded:(i + 1) * padded, :] = (
                    split(term)
                )
            total = dot3(wide_high[f], wide_low[f], rhs_high[...], rhs_low[...]) + damp * here
            if f == 1:
                total = total - pull
            res[...] = total
            res[:lowest, :] = res[:lowest, :] - low[f, y, :lowest, :]
            early = here - 0.5 * times(f, BI, res[...])
            for p in range(planes):
                out_lin[f, pl.ds(p * rows + y, moments, stride=cells), :] = early[
                    :moments, p * width:(p + 1) * width
                ]

    stores = []
    for f, target in enumerate((state_out, adjoint_out)):
        for side, y, slot in ((0, 0, HALO_PREV), (1, rows - 1, HALO_NEXT)):
            @pl.when(has["gy", side])
            def _(f=f, side=side):
                y_copy(f, 1 - side).wait_recv()

            late = times(f, slot, halo[f, side])
            for p in range(planes):
                spots = pl.ds(p * rows + y, moments, stride=cells)
                out_lin[f, spots, :] = (
                    out_lin[f, spots, :] + late[:moments, p * width:(p + 1) * width]
                )
        store = pltpu.make_async_copy(out_lin.at[f], target, out_sem.at[f])
        store.start()
        stores.append(store)

    for to in range(2):
        @pl.when(has["gx", to])
        def _(to=to):
            x_copy(to).wait_send()

        @pl.when(has["gy", to])
        def _(to=to):
            for f in range(2):
                y_copy(f, to).wait_send()
    for store in stores:
        store.wait()


def hand_over(pieces, a, b, a_out, b_out, sems):
    copies = []
    for f, (src, dst) in enumerate(((a, a_out), (b, b_out))):
        for i, (start, size) in enumerate(pieces):
            spots = pl.ds(start, size)
            copies.append(pltpu.make_async_copy(src.at[spots], dst.at[spots], sems.at[f, i]))
    for copy in copies:
        copy.start()
    for copy in copies:
        copy.wait()


def on_device(
    n_gx, n_gy, state, adjoint, upwind_pos, upwind_neg, collision, relax, wall_table,
    drag_weights, block_inverse, cell_codes, wall_mask,
):
    moments, planes, rows, width = state.shape
    lowest = collision.shape[0]
    assert planes == 2 and 2 * planes * rows <= width and lowest <= 64
    low_pad = -(-lowest // 8) * 8
    padded = -(-moments // 32) * 32
    flat = (moments * planes * rows, width)
    sizes = (moments, planes, rows, width, lowest, low_pad, padded, n_gx, n_gy)
    out = jax.ShapeDtypeStruct(flat, F32)
    anywhere = pl.BlockSpec(memory_space=pl.ANY)
    outs = pl.pallas_call(
        functools.partial(kernel, sizes),
        out_shape=(out, out),
        in_specs=[pl.BlockSpec(memory_space=pltpu.HBM)] * 11,
        out_specs=(anywhere, anywhere),
        scratch_shapes=[
            pltpu.VMEM((2,) + flat, F32),
            pltpu.VMEM(upwind_pos.shape, F32),
            pltpu.VMEM(upwind_neg.shape, F32),
            pltpu.VMEM(collision.shape, F32),
            pltpu.VMEM(relax.shape, F32),
            pltpu.VMEM(wall_table.shape, F32),
            pltpu.VMEM(drag_weights.shape, F32),
            pltpu.VMEM(block_inverse.shape, F32),
            pltpu.VMEM(cell_codes.shape, jnp.int32),
            pltpu.VMEM(wall_mask.shape, jnp.int32),
            pltpu.VMEM((2, rows, padded, planes * width), F32),
            pltpu.VMEM((2, padded, width), F32),
            pltpu.VMEM((2, padded, width), F32),
            pltpu.VMEM((2, 2, padded, planes * width), F32),
            pltpu.VMEM((padded, BLOCKS * padded), F32),
            pltpu.VMEM((2, padded, BLOCKS * padded), BF16),
            pltpu.VMEM((2, padded, BLOCKS * padded), BF16),
            pltpu.VMEM((padded, 3 * padded), F32),
            pltpu.VMEM((2, 3, padded, 3 * padded), BF16),
            pltpu.VMEM((BLOCKS * padded, planes * width), BF16),
            pltpu.VMEM((BLOCKS * padded, planes * width), BF16),
            pltpu.VMEM((lowest * low_pad, 128), F32),
            pltpu.VMEM((lowest * low_pad, planes * width), F32),
            pltpu.VMEM((2, rows, low_pad, planes * width), F32),
            pltpu.VMEM((padded, planes * width), F32),
            pltpu.VMEM((8, padded), F32),
            pltpu.VMEM((2,) + flat, F32),
            pltpu.SemaphoreType.DMA((11,)),
            pltpu.SemaphoreType.DMA((2,)),
            pltpu.SemaphoreType.DMA((2,)),
            pltpu.SemaphoreType.DMA((2,)),
            pltpu.SemaphoreType.DMA((2, 2)),
            pltpu.SemaphoreType.DMA((2, 2)),
        ],
        compiler_params=pltpu.CompilerParams(
            collective_id=0, has_side_effects=True, vmem_limit_bytes=64 * 1024 * 1024
        ),
    )(
        state.reshape(flat), adjoint.reshape(flat), upwind_pos, upwind_neg, collision, relax,
        wall_table, drag_weights, block_inverse, cell_codes, wall_mask,
    )
    step = -(-flat[0] // (8 * PIECES)) * 8
    pieces = [(at, min(step, flat[0] - at)) for at in range(0, flat[0], step)]
    outs = pl.pallas_call(
        functools.partial(hand_over, pieces),
        out_shape=(out, out),
        in_specs=[anywhere] * 2,
        out_specs=(anywhere, anywhere),
        scratch_shapes=[pltpu.SemaphoreType.DMA((2, len(pieces)))],
        compiler_params=pltpu.CompilerParams(vmem_limit_bytes=64 * 1024 * 1024),
    )(*outs)
    return tuple(o.reshape(state.shape) for o in outs)


def solution(mesh):
    in_specs = (
        P(None, None, "gy", "gx"),
        P(None, None, "gy", "gx"),
        P(),
        P(),
        P(),
        P(),
        P(),
        P(),
        P(),
        P(None, "gy", "gx"),
        P(None, "gy", "gx"),
    )
    out_specs = (P(None, None, "gy", "gx"), P(None, None, "gy", "gx"))
    return jax.shard_map(
        functools.partial(on_device, mesh.shape["gx"], mesh.shape["gy"]),
        mesh=mesh, in_specs=in_specs, out_specs=out_specs, check_vma=False,
    )
```

```python
import functools
import jax
import jax.numpy as jnp
from jax import lax
from jax.experimental import pallas as pl
from jax.experimental.pallas import tpu as pltpu
from jax.sharding import PartitionSpec as P

F32 = jnp.float32
BF16 = jnp.bfloat16
MESH = pl.DeviceIdType.MESH

PX, NX, PY, NY, DZ = range(5)
BLOCKS = 5
BI, HALO_PREV, HALO_NEXT = range(3)


def split(x):
    high = x.astype(BF16)
    return high, (x - high.astype(F32)).astype(BF16)


def dot(a, b):
    return jnp.dot(a, b, preferred_element_type=F32)


def dot3(a_high, a_low, b_high, b_low):
    return dot(a_high, b_high) + (dot(a_high, b_low) + dot(a_low, b_high))


def kernel(
    sizes,
    state, adjoint, pos, neg, coll, relax, table, drag, inverse, codes, walls,
    state_out, adjoint_out,
    lin, pos_v, neg_v, coll_v, relax_v, table_v, drag_v, inv_v, codes_v, walls_v,
    field, xsend, xrecv, halo, wide, wide_high, wide_low, tri, tri_b, rhs_high, rhs_low,
    sym, zed, low, res, vecs, out_lin,
    in_sem, out_sem, xs_sem, xr_sem, ys_sem, yr_sem,
):
    moments, planes, rows, width, lowest, low_pad, padded, n_gx, n_gy = sizes
    cells = planes * rows
    gx, gy = lax.axis_index("gx"), lax.axis_index("gy")
    has = {
        ("gx", 0): gx > 0, ("gx", 1): gx < n_gx - 1,
        ("gy", 0): gy > 0, ("gy", 1): gy < n_gy - 1,
    }
    where = {("gx", 0): gx - 1, ("gx", 1): gx + 1, ("gy", 0): gy - 1, ("gy", 1): gy + 1}

    loads = [
        pltpu.make_async_copy(src, dst, in_sem.at[i])
        for i, (src, dst) in enumerate(
            (
                (state, lin.at[0]), (adjoint, lin.at[1]), (coll, coll_v), (pos, pos_v),
                (neg, neg_v), (inverse, inv_v), (relax, relax_v), (table, table_v),
                (drag, drag_v), (codes, codes_v), (walls, walls_v),
            )
        )
    ]
    for load in loads:
        load.start()

    barrier = pltpu.get_barrier_semaphore()
    for side, there in has.items():
        @pl.when(there)
        def _(side=side):
            pl.semaphore_signal(
                barrier, inc=1, device_id={side[0]: where[side]}, device_id_type=MESH
            )
    field[:, :, moments:, :] = jnp.zeros((2, rows, padded - moments, planes * width), F32)
    pl.semaphore_wait(barrier, sum(there.astype(jnp.int32) for there in has.values()))

    def y_copy(f, to):
        return pltpu.make_async_remote_copy(
            src_ref=field.at[f, (rows - 1) * to],
            dst_ref=halo.at[f, 1 - to],
            send_sem=ys_sem.at[f, to],
            recv_sem=yr_sem.at[f, 1 - to],
            device_id={"gy": where["gy", to]},
            device_id_type=MESH,
        )

    def x_copy(to):
        return pltpu.make_async_remote_copy(
            src_ref=xsend.at[to],
            dst_ref=xrecv.at[1 - to],
            send_sem=xs_sem.at[to],
            recv_sem=xr_sem.at[1 - to],
            device_id={"gx": where["gx", to]},
            device_id_type=MESH,
        )

    def send_rows(f):
        for to in range(2):
            @pl.when(has["gy", to])
            def _(to=to):
                y_copy(f, to).start()

    for f in range(2):
        loads[f].wait()
        for p in range(planes):
            for y in range(rows):
                field[f, y, :moments, p * width:(p + 1) * width] = lin[
                    f, pl.ds(p * rows + y, moments, stride=cells), :
                ]
        if f == 0:
            send_rows(f)

    lanes = lax.broadcasted_iota(jnp.int32, (padded, width), 1)
    firsts = jnp.zeros((padded, width), F32)
    lasts = jnp.zeros((padded, width), F32)
    for f in range(2):
        for p in range(planes):
            for y in range(rows):
                spot = f * cells + p * rows + y
                block = field[f, y, :, p * width:(p + 1) * width]
                firsts = jnp.where(lanes == spot, pltpu.roll(block, spot, 1), firsts)
                lasts = jnp.where(lanes == spot, pltpu.roll(block, spot + 1, 1), lasts)
    xsend[0] = firsts
    xsend[1] = lasts
    for to in range(2):
        @pl.when(has["gx", to])
        def _(to=to):
            x_copy(to).start()

        @pl.when(jnp.logical_not(has["gx", to]))
        def _(to=to):
            xrecv[to] = jnp.zeros((padded, width), F32)

        @pl.when(jnp.logical_not(has["gy", to]))
        def _(to=to):
            for f in range(2):
                halo[f, to] = jnp.zeros((padded, planes * width), F32)

    loads[2].wait()
    sym[...] = jnp.zeros(sym.shape, F32)
    for k in range(lowest):
        c = coll_v[k]
        sym[k * low_pad:k * low_pad + lowest, :lowest] = 0.5 * (c + c.T)
    half = sym.shape[1] // 2
    sym_all = sym[...]
    sym_top = sym_all.astype(BF16).astype(F32)
    sym_k = jnp.concatenate(
        [(sym_top + pltpu.roll(sym_top, half, 1)).astype(BF16), (sym_all - sym_top).astype(BF16)],
        axis=1,
    )
    for y in range(rows):
        s_low = field[0, y, :lowest, :]
        a_low = field[1, y, :lowest, :]
        s_pad = field[0, y, :half, :]
        keep_rows = lax.broadcasted_iota(jnp.int32, s_pad.shape, 0) < lowest
        s_high, s_rest = split(jnp.where(keep_rows, s_pad, 0.0))
        s_k = jnp.concatenate([s_high, s_rest, s_high, jnp.zeros_like(s_high)], axis=0)
        zed[...] = dot(sym_k, s_k)
        adgain = jnp.zeros(a_low.shape, F32)
        for k in range(lowest):
            z_k = zed[k * low_pad:k * low_pad + lowest, :]
            low[0, y, k:k + 1, :] = jnp.sum(z_k * s_low, axis=0, keepdims=True)
            adgain = adgain + z_k * a_low[k:k + 1, :]
        low[1, y, :lowest, :] = 2.0 * adgain

    send_rows(1)

    for load in loads[3:]:
        load.wait()

    wide[...] = jnp.zeros(wide.shape, F32)
    tri[...] = jnp.zeros(tri.shape, F32)
    originals = (pos_v[0], neg_v[0], pos_v[1], neg_v[1], pos_v[2] - neg_v[2])

    def keep(f, slot, matrix):
        top = matrix.astype(BF16).astype(F32)
        tri[:moments, :moments] = top
        tri[:moments, padded:padded + moments] = top
        tri[:moments, 2 * padded:2 * padded + moments] = matrix - top
        tri_b[f, slot] = tri[...].astype(BF16)

    def times(f, slot, x):
        high, rest = split(x)
        return dot(tri_b[f, slot], jnp.concatenate([high, rest, high], axis=0))

    for f in range(2):
        for i, matrix in enumerate(originals):
            wide[:moments, i * padded:i * padded + moments] = matrix if f == 0 else matrix.T
        wide_high[f], wide_low[f] = split(wide[...])
        inv = inv_v[...] if f == 0 else inv_v[...].T
        inv_high, inv_low = split(inv)
        keep(f, BI, inv)
        for slot, block, scale in (
            (HALO_PREV, PY if f == 0 else NY, 0.5 if f == 0 else -0.5),
            (HALO_NEXT, NY if f == 0 else PY, -0.5 if f == 0 else 0.5),
        ):
            matrix = originals[block] if f == 0 else originals[block].T
            keep(f, slot, scale * dot3(inv_high, inv_low, *split(matrix)))

    vecs[...] = jnp.zeros(vecs.shape, F32)
    vecs[0:3, :moments] = table_v[...]
    vecs[3:4, :moments] = relax_v[...].reshape(1, moments)
    vecs[4:5, :moments] = drag_v[...].reshape(1, moments)
    whole = vecs[...]
    part1 = whole.astype(BF16).astype(F32)
    part2 = (whole - part1).astype(BF16).astype(F32)
    part3 = whole - part1 - part2
    parts = jnp.concatenate([part1, part2, part3], axis=0).T.astype(BF16)

    def spread(flags):
        return dot(parts, jnp.concatenate([flags] * 3, axis=0).astype(BF16))

    for to in range(2):
        @pl.when(has["gx", to])
        def _(to=to):
            x_copy(1 - to).wait_recv()

    kinds = lax.broadcasted_iota(jnp.int32, (8, width), 0)
    for y in range(rows):
        ones, marks = [], []
        for p in range(planes):
            code = codes_v[p, y:y + 1, :]
            ones.append(jnp.where(
                kinds < 3, (code == kinds + 1).astype(F32), (kinds == 3).astype(F32)))
            wall = walls_v[p, y:y + 1, :].astype(F32)
            marks.append(jnp.where(kinds == 4, wall, 0.0))
        damp = spread(jnp.concatenate(ones, axis=1))
        pull = spread(jnp.concatenate(marks, axis=1))
        for f in range(2):
            here = field[f, y]
            minus, plus = [], []
            for p in range(planes):
                spot = f * cells + p * rows + y
                block = here[:, p * width:(p + 1) * width]
                minus.append(jnp.where(
                    lanes == 0, xrecv[0, :, spot:spot + 1], pltpu.roll(block, 1, 1)))
                plus.append(jnp.where(
                    lanes == width - 1, xrecv[1, :, spot:spot + 1],
                    pltpu.roll(block, width - 1, 1)))
            x_minus = here - jnp.concatenate(minus, axis=1)
            x_plus = jnp.concatenate(plus, axis=1) - here
            y_minus = here - field[f, y - 1] if y > 0 else here
            y_plus = field[f, y + 1] - here if y < rows - 1 else -here
            z_diff = here[:, :width] - here[:, width:]
            z_both = jnp.concatenate([z_diff, -z_diff], axis=1)
            if f == 0:
                terms = (x_minus, x_plus, y_minus, y_plus, z_both)
            else:
                terms = (-x_plus, -x_minus, -y_plus, -y_minus, z_both)
            for i, term in enumerate(terms):
                rhs_high[i * padded:(i + 1) * padded, :], rhs_low[i * padded:(i + 1) * padded, :] = (
                    split(term)
                )
            total = dot3(wide_high[f], wide_low[f], rhs_high[...], rhs_low[...]) + damp * here
            if f == 1:
                total = total - pull
            res[...] = total
            res[:lowest, :] = res[:lowest, :] - low[f, y, :lowest, :]
            early = here - 0.5 * times(f, BI, res[...])
            for p in range(planes):
                out_lin[f, pl.ds(p * rows + y, moments, stride=cells), :] = early[
                    :moments, p * width:(p + 1) * width
                ]

    stores = []
    for f, target in enumerate((state_out, adjoint_out)):
        for side, y, slot in ((0, 0, HALO_PREV), (1, rows - 1, HALO_NEXT)):
            @pl.when(has["gy", side])
            def _(f=f, side=side):
                y_copy(f, 1 - side).wait_recv()

            late = times(f, slot, halo[f, side])
            for p in range(planes):
                spots = pl.ds(p * rows + y, moments, stride=cells)
                out_lin[f, spots, :] = (
                    out_lin[f, spots, :] + late[:moments, p * width:(p + 1) * width]
                )
        store = pltpu.make_async_copy(out_lin.at[f], target, out_sem.at[f])
        store.start()
        stores.append(store)

    for to in range(2):
        @pl.when(has["gx", to])
        def _(to=to):
            x_copy(to).wait_send()

        @pl.when(has["gy", to])
        def _(to=to):
            for f in range(2):
                y_copy(f, to).wait_send()
    for store in stores:
        store.wait()


def on_device(
    n_gx, n_gy, state, adjoint, upwind_pos, upwind_neg, collision, relax, wall_table,
    drag_weights, block_inverse, cell_codes, wall_mask,
):
    moments, planes, rows, width = state.shape
    lowest = collision.shape[0]
    assert planes == 2 and 2 * planes * rows <= width and lowest <= 64
    low_pad = -(-lowest // 8) * 8
    padded = -(-moments // 32) * 32
    flat = (moments * planes * rows, width)
    sizes = (moments, planes, rows, width, lowest, low_pad, padded, n_gx, n_gy)
    out = jax.ShapeDtypeStruct(flat, F32)
    anywhere = pl.BlockSpec(memory_space=pl.ANY)
    outs = pl.pallas_call(
        functools.partial(kernel, sizes),
        out_shape=(out, out),
        in_specs=[pl.BlockSpec(memory_space=pltpu.HBM)] * 11,
        out_specs=(anywhere, anywhere),
        scratch_shapes=[
            pltpu.VMEM((2,) + flat, F32),
            pltpu.VMEM(upwind_pos.shape, F32),
            pltpu.VMEM(upwind_neg.shape, F32),
            pltpu.VMEM(collision.shape, F32),
            pltpu.VMEM(relax.shape, F32),
            pltpu.VMEM(wall_table.shape, F32),
            pltpu.VMEM(drag_weights.shape, F32),
            pltpu.VMEM(block_inverse.shape, F32),
            pltpu.VMEM(cell_codes.shape, jnp.int32),
            pltpu.VMEM(wall_mask.shape, jnp.int32),
            pltpu.VMEM((2, rows, padded, planes * width), F32),
            pltpu.VMEM((2, padded, width), F32),
            pltpu.VMEM((2, padded, width), F32),
            pltpu.VMEM((2, 2, padded, planes * width), F32),
            pltpu.VMEM((padded, BLOCKS * padded), F32),
            pltpu.VMEM((2, padded, BLOCKS * padded), BF16),
            pltpu.VMEM((2, padded, BLOCKS * padded), BF16),
            pltpu.VMEM((padded, 3 * padded), F32),
            pltpu.VMEM((2, 3, padded, 3 * padded), BF16),
            pltpu.VMEM((BLOCKS * padded, planes * width), BF16),
            pltpu.VMEM((BLOCKS * padded, planes * width), BF16),
            pltpu.VMEM((lowest * low_pad, 128), F32),
            pltpu.VMEM((lowest * low_pad, planes * width), F32),
            pltpu.VMEM((2, rows, low_pad, planes * width), F32),
            pltpu.VMEM((padded, planes * width), F32),
            pltpu.VMEM((8, padded), F32),
            pltpu.VMEM((2,) + flat, F32),
            pltpu.SemaphoreType.DMA((11,)),
            pltpu.SemaphoreType.DMA((2,)),
            pltpu.SemaphoreType.DMA((2,)),
            pltpu.SemaphoreType.DMA((2,)),
            pltpu.SemaphoreType.DMA((2, 2)),
            pltpu.SemaphoreType.DMA((2, 2)),
        ],
        compiler_params=pltpu.CompilerParams(
            collective_id=0, has_side_effects=True, vmem_limit_bytes=64 * 1024 * 1024
        ),
    )(
        state.reshape(flat), adjoint.reshape(flat), upwind_pos, upwind_neg, collision, relax,
        wall_table, drag_weights, block_inverse, cell_codes, wall_mask,
    )
    return tuple(o.reshape(state.shape) for o in outs)


def solution(mesh):
    in_specs = (
        P(None, None, "gy", "gx"),
        P(None, None, "gy", "gx"),
        P(),
        P(),
        P(),
        P(),
        P(),
        P(),
        P(),
        P(None, "gy", "gx"),
        P(None, "gy", "gx"),
    )
    out_specs = (P(None, None, "gy", "gx"), P(None, None, "gy", "gx"))
    return jax.shard_map(
        functools.partial(on_device, mesh.shape["gx"], mesh.shape["gy"]),
        mesh=mesh, in_specs=in_specs, out_specs=out_specs, check_vma=False,
    )
```

```python
import functools
import jax
import jax.numpy as jnp
from jax import lax
from jax.experimental import pallas as pl
from jax.experimental.pallas import tpu as pltpu
from jax.sharding import PartitionSpec as P

F32 = jnp.float32
BF16 = jnp.bfloat16
MESH = pl.DeviceIdType.MESH

PX, NX, PY, NY, DZ = range(5)
BLOCKS = 5
PIECES = 2
BI, HALO_PREV, HALO_NEXT = range(3)


def split(x):
    high = x.astype(BF16)
    return high, (x - high.astype(F32)).astype(BF16)


def dot(a, b):
    return jnp.dot(a, b, preferred_element_type=F32)


def dot3(a_high, a_low, b_high, b_low):
    return dot(a_high, b_high) + (dot(a_high, b_low) + dot(a_low, b_high))


def kernel(
    sizes,
    state, adjoint, pos, neg, coll, relax, table, drag, inverse, codes, walls,
    state_out, adjoint_out,
    lin, pos_v, neg_v, coll_v, relax_v, table_v, drag_v, inv_v, codes_v, walls_v,
    field, xsend, xrecv, halo, wide, wide_high, wide_low, tri, tri_b, rhs_high, rhs_low,
    sym, zed, low, res, vecs, out_lin,
    in_sem, out_sem, xs_sem, xr_sem, ys_sem, yr_sem,
):
    moments, planes, rows, width, lowest, low_pad, padded, n_gx, n_gy = sizes
    cells = planes * rows
    gx, gy = lax.axis_index("gx"), lax.axis_index("gy")
    has = {
        ("gx", 0): gx > 0, ("gx", 1): gx < n_gx - 1,
        ("gy", 0): gy > 0, ("gy", 1): gy < n_gy - 1,
    }
    where = {("gx", 0): gx - 1, ("gx", 1): gx + 1, ("gy", 0): gy - 1, ("gy", 1): gy + 1}

    loads = [
        pltpu.make_async_copy(src, dst, in_sem.at[i])
        for i, (src, dst) in enumerate(
            (
                (state, lin.at[0]), (adjoint, lin.at[1]), (coll, coll_v), (pos, pos_v),
                (neg, neg_v), (inverse, inv_v), (relax, relax_v), (table, table_v),
                (drag, drag_v), (codes, codes_v), (walls, walls_v),
            )
        )
    ]
    for load in loads:
        load.start()

    barrier = pltpu.get_barrier_semaphore()
    for side, there in has.items():
        @pl.when(there)
        def _(side=side):
            pl.semaphore_signal(
                barrier, inc=1, device_id={side[0]: where[side]}, device_id_type=MESH
            )
    field[:, :, moments:, :] = jnp.zeros((2, rows, padded - moments, planes * width), F32)
    pl.semaphore_wait(barrier, sum(there.astype(jnp.int32) for there in has.values()))

    def y_copy(f, to):
        return pltpu.make_async_remote_copy(
            src_ref=field.at[f, (rows - 1) * to],
            dst_ref=halo.at[f, 1 - to],
            send_sem=ys_sem.at[f, to],
            recv_sem=yr_sem.at[f, 1 - to],
            device_id={"gy": where["gy", to]},
            device_id_type=MESH,
        )

    def x_copy(to):
        return pltpu.make_async_remote_copy(
            src_ref=xsend.at[to],
            dst_ref=xrecv.at[1 - to],
            send_sem=xs_sem.at[to],
            recv_sem=xr_sem.at[1 - to],
            device_id={"gx": where["gx", to]},
            device_id_type=MESH,
        )

    parity = lax.rem(gy, 2)

    def send_rows(f, first):
        for to in range(2):
            turn = parity == to if first else parity != to

            @pl.when(jnp.logical_and(has["gy", to], turn))
            def _(to=to):
                y_copy(f, to).start()

    for f in range(2):
        loads[f].wait()
        for p in range(planes):
            for y in range(rows):
                field[f, y, :moments, p * width:(p + 1) * width] = lin[
                    f, pl.ds(p * rows + y, moments, stride=cells), :
                ]
        send_rows(f, True)

    lanes = lax.broadcasted_iota(jnp.int32, (padded, width), 1)
    firsts = jnp.zeros((padded, width), F32)
    lasts = jnp.zeros((padded, width), F32)
    for f in range(2):
        for p in range(planes):
            for y in range(rows):
                spot = f * cells + p * rows + y
                block = field[f, y, :, p * width:(p + 1) * width]
                firsts = jnp.where(lanes == spot, pltpu.roll(block, spot, 1), firsts)
                lasts = jnp.where(lanes == spot, pltpu.roll(block, spot + 1, 1), lasts)
    xsend[0] = firsts
    xsend[1] = lasts
    for to in range(2):
        @pl.when(has["gx", to])
        def _(to=to):
            x_copy(to).start()

        @pl.when(jnp.logical_not(has["gx", to]))
        def _(to=to):
            xrecv[to] = jnp.zeros((padded, width), F32)

        @pl.when(jnp.logical_not(has["gy", to]))
        def _(to=to):
            for f in range(2):
                halo[f, to] = jnp.zeros((padded, planes * width), F32)

    loads[2].wait()
    sym[...] = jnp.zeros(sym.shape, F32)
    for k in range(lowest):
        c = coll_v[k]
        sym[k * low_pad:k * low_pad + lowest, :lowest] = 0.5 * (c + c.T)
    half = sym.shape[1] // 2
    sym_all = sym[...]
    sym_top = sym_all.astype(BF16).astype(F32)
    sym_k = jnp.concatenate(
        [(sym_top + pltpu.roll(sym_top, half, 1)).astype(BF16), (sym_all - sym_top).astype(BF16)],
        axis=1,
    )
    for y in range(rows):
        s_low = field[0, y, :lowest, :]
        a_low = field[1, y, :lowest, :]
        s_pad = field[0, y, :half, :]
        keep_rows = lax.broadcasted_iota(jnp.int32, s_pad.shape, 0) < lowest
        s_high, s_rest = split(jnp.where(keep_rows, s_pad, 0.0))
        s_k = jnp.concatenate([s_high, s_rest, s_high, jnp.zeros_like(s_high)], axis=0)
        zed[...] = dot(sym_k, s_k)
        adgain = jnp.zeros(a_low.shape, F32)
        for k in range(lowest):
            z_k = zed[k * low_pad:k * low_pad + lowest, :]
            low[0, y, k:k + 1, :] = jnp.sum(z_k * s_low, axis=0, keepdims=True)
            adgain = adgain + z_k * a_low[k:k + 1, :]
        low[1, y, :lowest, :] = 2.0 * adgain

    for f in range(2):
        send_rows(f, False)

    for load in loads[3:]:
        load.wait()

    wide[...] = jnp.zeros(wide.shape, F32)
    tri[...] = jnp.zeros(tri.shape, F32)
    originals = (pos_v[0], neg_v[0], pos_v[1], neg_v[1], pos_v[2] - neg_v[2])

    def keep(f, slot, matrix):
        top = matrix.astype(BF16).astype(F32)
        tri[:moments, :moments] = top
        tri[:moments, padded:padded + moments] = top
        tri[:moments, 2 * padded:2 * padded + moments] = matrix - top
        tri_b[f, slot] = tri[...].astype(BF16)

    def times(f, slot, x):
        high, rest = split(x)
        return dot(tri_b[f, slot], jnp.concatenate([high, rest, high], axis=0))

    for f in range(2):
        for i, matrix in enumerate(originals):
            wide[:moments, i * padded:i * padded + moments] = matrix if f == 0 else matrix.T
        wide_high[f], wide_low[f] = split(wide[...])
        inv = inv_v[...] if f == 0 else inv_v[...].T
        inv_high, inv_low = split(inv)
        keep(f, BI, inv)
        for slot, block, scale in (
            (HALO_PREV, PY if f == 0 else NY, 0.5 if f == 0 else -0.5),
            (HALO_NEXT, NY if f == 0 else PY, -0.5 if f == 0 else 0.5),
        ):
            matrix = originals[block] if f == 0 else originals[block].T
            keep(f, slot, scale * dot3(inv_high, inv_low, *split(matrix)))

    vecs[...] = jnp.zeros(vecs.shape, F32)
    vecs[0:3, :moments] = table_v[...]
    vecs[3:4, :moments] = relax_v[...].reshape(1, moments)
    vecs[4:5, :moments] = drag_v[...].reshape(1, moments)
    whole = vecs[...]
    part1 = whole.astype(BF16).astype(F32)
    part2 = (whole - part1).astype(BF16).astype(F32)
    part3 = whole - part1 - part2
    parts = jnp.concatenate([part1, part2, part3], axis=0).T.astype(BF16)

    def spread(flags):
        return dot(parts, jnp.concatenate([flags] * 3, axis=0).astype(BF16))

    for to in range(2):
        @pl.when(has["gx", to])
        def _(to=to):
            x_copy(1 - to).wait_recv()

    kinds = lax.broadcasted_iota(jnp.int32, (8, width), 0)
    for y in range(rows):
        ones, marks = [], []
        for p in range(planes):
            code = codes_v[p, y:y + 1, :]
            ones.append(jnp.where(
                kinds < 3, (code == kinds + 1).astype(F32), (kinds == 3).astype(F32)))
            wall = walls_v[p, y:y + 1, :].astype(F32)
            marks.append(jnp.where(kinds == 4, wall, 0.0))
        damp = spread(jnp.concatenate(ones, axis=1))
        pull = spread(jnp.concatenate(marks, axis=1))
        for f in range(2):
            here = field[f, y]
            minus, plus = [], []
            for p in range(planes):
                spot = f * cells + p * rows + y
                block = here[:, p * width:(p + 1) * width]
                minus.append(jnp.where(
                    lanes == 0, xrecv[0, :, spot:spot + 1], pltpu.roll(block, 1, 1)))
                plus.append(jnp.where(
                    lanes == width - 1, xrecv[1, :, spot:spot + 1],
                    pltpu.roll(block, width - 1, 1)))
            x_minus = here - jnp.concatenate(minus, axis=1)
            x_plus = jnp.concatenate(plus, axis=1) - here
            y_minus = here - field[f, y - 1] if y > 0 else here
            y_plus = field[f, y + 1] - here if y < rows - 1 else -here
            z_diff = here[:, :width] - here[:, width:]
            z_both = jnp.concatenate([z_diff, -z_diff], axis=1)
            if f == 0:
                terms = (x_minus, x_plus, y_minus, y_plus, z_both)
            else:
                terms = (-x_plus, -x_minus, -y_plus, -y_minus, z_both)
            for i, term in enumerate(terms):
                rhs_high[i * padded:(i + 1) * padded, :], rhs_low[i * padded:(i + 1) * padded, :] = (
                    split(term)
                )
            total = dot3(wide_high[f], wide_low[f], rhs_high[...], rhs_low[...]) + damp * here
            if f == 1:
                total = total - pull
            res[...] = total
            res[:lowest, :] = res[:lowest, :] - low[f, y, :lowest, :]
            early = here - 0.5 * times(f, BI, res[...])
            for p in range(planes):
                out_lin[f, pl.ds(p * rows + y, moments, stride=cells), :] = early[
                    :moments, p * width:(p + 1) * width
                ]

    stores = [
        pltpu.make_async_copy(out_lin.at[f], target, out_sem.at[f])
        for f, target in enumerate((state_out, adjoint_out))
    ]

    def finish(f, side):
        y, slot = ((0, HALO_PREV), (rows - 1, HALO_NEXT))[side]

        @pl.when(has["gy", side])
        def _():
            y_copy(f, 1 - side).wait_recv()

        late = times(f, slot, halo[f, side])
        for p in range(planes):
            spots = pl.ds(p * rows + y, moments, stride=cells)
            out_lin[f, spots, :] = (
                out_lin[f, spots, :] + late[:moments, p * width:(p + 1) * width]
            )

    for side in range(2):
        @pl.when(parity == side)
        def _(side=side):
            for f in range(2):
                finish(f, side)
            for f in range(2):
                finish(f, 1 - side)
                stores[f].start()

    for to in range(2):
        @pl.when(has["gx", to])
        def _(to=to):
            x_copy(to).wait_send()

        @pl.when(has["gy", to])
        def _(to=to):
            for f in range(2):
                y_copy(f, to).wait_send()
    for store in stores:
        store.wait()


def hand_over(pieces, a, b, a_out, b_out, held, in_sems, out_sems):
    ins, outs = [], []
    for f, (src, dst) in enumerate(((a, a_out), (b, b_out))):
        for i, (start, size) in enumerate(pieces):
            spots = pl.ds(start, size)
            ins.append(pltpu.make_async_copy(
                src.at[spots], held.at[f, spots], in_sems.at[f, i]))
            outs.append(pltpu.make_async_copy(
                held.at[f, spots], dst.at[spots], out_sems.at[f, i]))
    for copy in ins:
        copy.start()
    for arrived, leaving in zip(ins, outs):
        arrived.wait()
        leaving.start()
    for copy in outs:
        copy.wait()


def on_device(
    n_gx, n_gy, state, adjoint, upwind_pos, upwind_neg, collision, relax, wall_table,
    drag_weights, block_inverse, cell_codes, wall_mask,
):
    moments, planes, rows, width = state.shape
    lowest = collision.shape[0]
    assert planes == 2 and 2 * planes * rows <= width and lowest <= 64
    low_pad = -(-lowest // 8) * 8
    padded = -(-moments // 32) * 32
    flat = (moments * planes * rows, width)
    sizes = (moments, planes, rows, width, lowest, low_pad, padded, n_gx, n_gy)
    out = jax.ShapeDtypeStruct(flat, F32)
    anywhere = pl.BlockSpec(memory_space=pl.ANY)
    outs = pl.pallas_call(
        functools.partial(kernel, sizes),
        out_shape=(out, out),
        in_specs=[pl.BlockSpec(memory_space=pltpu.HBM)] * 11,
        out_specs=(anywhere, anywhere),
        scratch_shapes=[
            pltpu.VMEM((2,) + flat, F32),
            pltpu.VMEM(upwind_pos.shape, F32),
            pltpu.VMEM(upwind_neg.shape, F32),
            pltpu.VMEM(collision.shape, F32),
            pltpu.VMEM(relax.shape, F32),
            pltpu.VMEM(wall_table.shape, F32),
            pltpu.VMEM(drag_weights.shape, F32),
            pltpu.VMEM(block_inverse.shape, F32),
            pltpu.VMEM(cell_codes.shape, jnp.int32),
            pltpu.VMEM(wall_mask.shape, jnp.int32),
            pltpu.VMEM((2, rows, padded, planes * width), F32),
            pltpu.VMEM((2, padded, width), F32),
            pltpu.VMEM((2, padded, width), F32),
            pltpu.VMEM((2, 2, padded, planes * width), F32),
            pltpu.VMEM((padded, BLOCKS * padded), F32),
            pltpu.VMEM((2, padded, BLOCKS * padded), BF16),
            pltpu.VMEM((2, padded, BLOCKS * padded), BF16),
            pltpu.VMEM((padded, 3 * padded), F32),
            pltpu.VMEM((2, 3, padded, 3 * padded), BF16),
            pltpu.VMEM((BLOCKS * padded, planes * width), BF16),
            pltpu.VMEM((BLOCKS * padded, planes * width), BF16),
            pltpu.VMEM((lowest * low_pad, 128), F32),
            pltpu.VMEM((lowest * low_pad, planes * width), F32),
            pltpu.VMEM((2, rows, low_pad, planes * width), F32),
            pltpu.VMEM((padded, planes * width), F32),
            pltpu.VMEM((8, padded), F32),
            pltpu.VMEM((2,) + flat, F32),
            pltpu.SemaphoreType.DMA((11,)),
            pltpu.SemaphoreType.DMA((2,)),
            pltpu.SemaphoreType.DMA((2,)),
            pltpu.SemaphoreType.DMA((2,)),
            pltpu.SemaphoreType.DMA((2, 2)),
            pltpu.SemaphoreType.DMA((2, 2)),
        ],
        compiler_params=pltpu.CompilerParams(
            collective_id=0, has_side_effects=True, vmem_limit_bytes=64 * 1024 * 1024
        ),
    )(
        state.reshape(flat), adjoint.reshape(flat), upwind_pos, upwind_neg, collision, relax,
        wall_table, drag_weights, block_inverse, cell_codes, wall_mask,
    )
    step = -(-flat[0] // (8 * PIECES)) * 8
    pieces = [(at, min(step, flat[0] - at)) for at in range(0, flat[0], step)]
    outs = pl.pallas_call(
        functools.partial(hand_over, pieces),
        out_shape=(out, out),
        in_specs=[anywhere] * 2,
        out_specs=(anywhere, anywhere),
        scratch_shapes=[
            pltpu.VMEM((2,) + flat, F32),
            pltpu.SemaphoreType.DMA((2, len(pieces))),
            pltpu.SemaphoreType.DMA((2, len(pieces))),
        ],
        compiler_params=pltpu.CompilerParams(vmem_limit_bytes=64 * 1024 * 1024),
    )(*outs)
    return tuple(o.reshape(state.shape) for o in outs)


def solution(mesh):
    in_specs = (
        P(None, None, "gy", "gx"),
        P(None, None, "gy", "gx"),
        P(),
        P(),
        P(),
        P(),
        P(),
        P(),
        P(),
        P(None, "gy", "gx"),
        P(None, "gy", "gx"),
    )
    out_specs = (P(None, None, "gy", "gx"), P(None, None, "gy", "gx"))
    return jax.shard_map(
        functools.partial(on_device, mesh.shape["gx"], mesh.shape["gy"]),
        mesh=mesh, in_specs=in_specs, out_specs=out_specs, check_vma=False,
    )
```

```python
import functools
import jax
import jax.numpy as jnp
from jax import lax
from jax.experimental import pallas as pl
from jax.experimental.pallas import tpu as pltpu
from jax.sharding import PartitionSpec as P

F32 = jnp.float32
BF16 = jnp.bfloat16
MESH = pl.DeviceIdType.MESH

PX, NX, PY, NY, DZ = range(5)
BLOCKS = 5
PIECES = 2
BI, HALO_PREV, HALO_NEXT = range(3)


def split(x):
    high = x.astype(BF16)
    return high, (x - high.astype(F32)).astype(BF16)


def dot(a, b):
    return jnp.dot(a, b, preferred_element_type=F32)


def dot3(a_high, a_low, b_high, b_low):
    return dot(a_high, b_high) + (dot(a_high, b_low) + dot(a_low, b_high))


def kernel(
    sizes,
    state, adjoint, pos, neg, coll, relax, table, drag, inverse, codes, walls,
    state_out, adjoint_out,
    lin, pos_v, neg_v, coll_v, relax_v, table_v, drag_v, inv_v, codes_v, walls_v,
    field, xsend, xrecv, halo, wide, wide_high, wide_low, tri, tri_b, rhs_high, rhs_low,
    sym, zed, low, res, vecs, out_lin,
    in_sem, out_sem, xs_sem, xr_sem, ys_sem, yr_sem,
):
    moments, planes, rows, width, lowest, low_pad, padded, n_gx, n_gy = sizes
    cells = planes * rows
    gx, gy = lax.axis_index("gx"), lax.axis_index("gy")
    has = {
        ("gx", 0): gx > 0, ("gx", 1): gx < n_gx - 1,
        ("gy", 0): gy > 0, ("gy", 1): gy < n_gy - 1,
    }
    where = {("gx", 0): gx - 1, ("gx", 1): gx + 1, ("gy", 0): gy - 1, ("gy", 1): gy + 1}

    loads = [
        pltpu.make_async_copy(src, dst, in_sem.at[i])
        for i, (src, dst) in enumerate(
            (
                (state, lin.at[0]), (adjoint, lin.at[1]), (coll, coll_v), (pos, pos_v),
                (neg, neg_v), (inverse, inv_v), (relax, relax_v), (table, table_v),
                (drag, drag_v), (codes, codes_v), (walls, walls_v),
            )
        )
    ]
    for load in loads:
        load.start()

    barrier = pltpu.get_barrier_semaphore()
    for side, there in has.items():
        @pl.when(there)
        def _(side=side):
            pl.semaphore_signal(
                barrier, inc=1, device_id={side[0]: where[side]}, device_id_type=MESH
            )
    field[:, :, moments:, :] = jnp.zeros((2, rows, padded - moments, planes * width), F32)
    pl.semaphore_wait(barrier, sum(there.astype(jnp.int32) for there in has.values()))

    def y_copy(f, to):
        return pltpu.make_async_remote_copy(
            src_ref=field.at[f, (rows - 1) * to],
            dst_ref=halo.at[f, 1 - to],
            send_sem=ys_sem.at[f, to],
            recv_sem=yr_sem.at[f, 1 - to],
            device_id={"gy": where["gy", to]},
            device_id_type=MESH,
        )

    def x_copy(to):
        return pltpu.make_async_remote_copy(
            src_ref=xsend.at[to],
            dst_ref=xrecv.at[1 - to],
            send_sem=xs_sem.at[to],
            recv_sem=xr_sem.at[1 - to],
            device_id={"gx": where["gx", to]},
            device_id_type=MESH,
        )

    parity = lax.rem(gy, 2)

    def send_rows(f, first):
        for to in range(2):
            turn = parity == to if first else parity != to

            @pl.when(jnp.logical_and(has["gy", to], turn))
            def _(to=to):
                y_copy(f, to).start()

    for f in range(2):
        loads[f].wait()
        for p in range(planes):
            for y in range(rows):
                field[f, y, :moments, p * width:(p + 1) * width] = lin[
                    f, pl.ds(p * rows + y, moments, stride=cells), :
                ]
        send_rows(f, True)

    for f in range(2):
        send_rows(f, False)

    lanes = lax.broadcasted_iota(jnp.int32, (padded, width), 1)
    firsts = jnp.zeros((padded, width), F32)
    lasts = jnp.zeros((padded, width), F32)
    for f in range(2):
        for p in range(planes):
            for y in range(rows):
                spot = f * cells + p * rows + y
                block = field[f, y, :, p * width:(p + 1) * width]
                firsts = jnp.where(lanes == spot, pltpu.roll(block, spot, 1), firsts)
                lasts = jnp.where(lanes == spot, pltpu.roll(block, spot + 1, 1), lasts)
    xsend[0] = firsts
    xsend[1] = lasts
    for to in range(2):
        @pl.when(has["gx", to])
        def _(to=to):
            x_copy(to).start()

        @pl.when(jnp.logical_not(has["gx", to]))
        def _(to=to):
            xrecv[to] = jnp.zeros((padded, width), F32)

        @pl.when(jnp.logical_not(has["gy", to]))
        def _(to=to):
            for f in range(2):
                halo[f, to] = jnp.zeros((padded, planes * width), F32)

    loads[2].wait()
    sym[...] = jnp.zeros(sym.shape, F32)
    for k in range(lowest):
        c = coll_v[k]
        sym[k * low_pad:k * low_pad + lowest, :lowest] = 0.5 * (c + c.T)
    half = sym.shape[1] // 2
    sym_all = sym[...]
    sym_top = sym_all.astype(BF16).astype(F32)
    sym_k = jnp.concatenate(
        [(sym_top + pltpu.roll(sym_top, half, 1)).astype(BF16), (sym_all - sym_top).astype(BF16)],
        axis=1,
    )
    for y in range(rows):
        s_low = field[0, y, :lowest, :]
        a_low = field[1, y, :lowest, :]
        s_pad = field[0, y, :half, :]
        keep_rows = lax.broadcasted_iota(jnp.int32, s_pad.shape, 0) < lowest
        s_high, s_rest = split(jnp.where(keep_rows, s_pad, 0.0))
        s_k = jnp.concatenate([s_high, s_rest, s_high, jnp.zeros_like(s_high)], axis=0)
        zed[...] = dot(sym_k, s_k)
        adgain = jnp.zeros(a_low.shape, F32)
        for k in range(lowest):
            z_k = zed[k * low_pad:k * low_pad + lowest, :]
            low[0, y, k:k + 1, :] = jnp.sum(z_k * s_low, axis=0, keepdims=True)
            adgain = adgain + z_k * a_low[k:k + 1, :]
        low[1, y, :lowest, :] = 2.0 * adgain

    for load in loads[3:]:
        load.wait()

    wide[...] = jnp.zeros(wide.shape, F32)
    tri[...] = jnp.zeros(tri.shape, F32)
    originals = (pos_v[0], neg_v[0], pos_v[1], neg_v[1], pos_v[2] - neg_v[2])

    def keep(f, slot, matrix):
        top = matrix.astype(BF16).astype(F32)
        tri[:moments, :moments] = top
        tri[:moments, padded:padded + moments] = top
        tri[:moments, 2 * padded:2 * padded + moments] = matrix - top
        tri_b[f, slot] = tri[...].astype(BF16)

    def times(f, slot, x):
        high, rest = split(x)
        return dot(tri_b[f, slot], jnp.concatenate([high, rest, high], axis=0))

    for f in range(2):
        for i, matrix in enumerate(originals):
            wide[:moments, i * padded:i * padded + moments] = matrix if f == 0 else matrix.T
        wide_high[f], wide_low[f] = split(wide[...])
        inv = inv_v[...] if f == 0 else inv_v[...].T
        inv_high, inv_low = split(inv)
        keep(f, BI, inv)
        for slot, block, scale in (
            (HALO_PREV, PY if f == 0 else NY, 0.5 if f == 0 else -0.5),
            (HALO_NEXT, NY if f == 0 else PY, -0.5 if f == 0 else 0.5),
        ):
            matrix = originals[block] if f == 0 else originals[block].T
            keep(f, slot, scale * dot3(inv_high, inv_low, *split(matrix)))

    vecs[...] = jnp.zeros(vecs.shape, F32)
    vecs[0:3, :moments] = table_v[...]
    vecs[3:4, :moments] = relax_v[...].reshape(1, moments)
    vecs[4:5, :moments] = drag_v[...].reshape(1, moments)
    whole = vecs[...]
    part1 = whole.astype(BF16).astype(F32)
    part2 = (whole - part1).astype(BF16).astype(F32)
    part3 = whole - part1 - part2
    parts = jnp.concatenate([part1, part2, part3], axis=0).T.astype(BF16)

    def spread(flags):
        return dot(parts, jnp.concatenate([flags] * 3, axis=0).astype(BF16))

    for to in range(2):
        @pl.when(has["gx", to])
        def _(to=to):
            x_copy(1 - to).wait_recv()

    kinds = lax.broadcasted_iota(jnp.int32, (8, width), 0)
    for y in range(rows):
        ones, marks = [], []
        for p in range(planes):
            code = codes_v[p, y:y + 1, :]
            ones.append(jnp.where(
                kinds < 3, (code == kinds + 1).astype(F32), (kinds == 3).astype(F32)))
            wall = walls_v[p, y:y + 1, :].astype(F32)
            marks.append(jnp.where(kinds == 4, wall, 0.0))
        damp = spread(jnp.concatenate(ones, axis=1))
        pull = spread(jnp.concatenate(marks, axis=1))
        for f in range(2):
            here = field[f, y]
            minus, plus = [], []
            for p in range(planes):
                spot = f * cells + p * rows + y
                block = here[:, p * width:(p + 1) * width]
                minus.append(jnp.where(
                    lanes == 0, xrecv[0, :, spot:spot + 1], pltpu.roll(block, 1, 1)))
                plus.append(jnp.where(
                    lanes == width - 1, xrecv[1, :, spot:spot + 1],
                    pltpu.roll(block, width - 1, 1)))
            x_minus = here - jnp.concatenate(minus, axis=1)
            x_plus = jnp.concatenate(plus, axis=1) - here
            y_minus = here - field[f, y - 1] if y > 0 else here
            y_plus = field[f, y + 1] - here if y < rows - 1 else -here
            z_diff = here[:, :width] - here[:, width:]
            z_both = jnp.concatenate([z_diff, -z_diff], axis=1)
            if f == 0:
                terms = (x_minus, x_plus, y_minus, y_plus, z_both)
            else:
                terms = (-x_plus, -x_minus, -y_plus, -y_minus, z_both)
            for i, term in enumerate(terms):
                rhs_high[i * padded:(i + 1) * padded, :], rhs_low[i * padded:(i + 1) * padded, :] = (
                    split(term)
                )
            total = dot3(wide_high[f], wide_low[f], rhs_high[...], rhs_low[...]) + damp * here
            if f == 1:
                total = total - pull
            res[...] = total
            res[:lowest, :] = res[:lowest, :] - low[f, y, :lowest, :]
            early = here - 0.5 * times(f, BI, res[...])
            for p in range(planes):
                out_lin[f, pl.ds(p * rows + y, moments, stride=cells), :] = early[
                    :moments, p * width:(p + 1) * width
                ]

    stores = [
        pltpu.make_async_copy(out_lin.at[f], target, out_sem.at[f])
        for f, target in enumerate((state_out, adjoint_out))
    ]

    def finish(f, side):
        y, slot = ((0, HALO_PREV), (rows - 1, HALO_NEXT))[side]

        @pl.when(has["gy", side])
        def _():
            y_copy(f, 1 - side).wait_recv()

        late = times(f, slot, halo[f, side])
        for p in range(planes):
            spots = pl.ds(p * rows + y, moments, stride=cells)
            out_lin[f, spots, :] = (
                out_lin[f, spots, :] + late[:moments, p * width:(p + 1) * width]
            )

    for side in range(2):
        @pl.when(parity == side)
        def _(side=side):
            for f in range(2):
                finish(f, side)
            for f in range(2):
                finish(f, 1 - side)
                stores[f].start()

    for to in range(2):
        @pl.when(has["gx", to])
        def _(to=to):
            x_copy(to).wait_send()

        @pl.when(has["gy", to])
        def _(to=to):
            for f in range(2):
                y_copy(f, to).wait_send()
    for store in stores:
        store.wait()


def hand_over(pieces, a, b, a_out, b_out, held, in_sems, out_sems):
    ins, outs = [], []
    for f, (src, dst) in enumerate(((a, a_out), (b, b_out))):
        for i, (start, size) in enumerate(pieces):
            spots = pl.ds(start, size)
            ins.append(pltpu.make_async_copy(
                src.at[spots], held.at[f, spots], in_sems.at[f, i]))
            outs.append(pltpu.make_async_copy(
                held.at[f, spots], dst.at[spots], out_sems.at[f, i]))
    for copy in ins:
        copy.start()
    for arrived, leaving in zip(ins, outs):
        arrived.wait()
        leaving.start()
    for copy in outs:
        copy.wait()


def on_device(
    n_gx, n_gy, state, adjoint, upwind_pos, upwind_neg, collision, relax, wall_table,
    drag_weights, block_inverse, cell_codes, wall_mask,
):
    moments, planes, rows, width = state.shape
    lowest = collision.shape[0]
    assert planes == 2 and 2 * planes * rows <= width and lowest <= 64
    low_pad = -(-lowest // 8) * 8
    padded = -(-moments // 32) * 32
    flat = (moments * planes * rows, width)
    sizes = (moments, planes, rows, width, lowest, low_pad, padded, n_gx, n_gy)
    out = jax.ShapeDtypeStruct(flat, F32)
    anywhere = pl.BlockSpec(memory_space=pl.ANY)
    outs = pl.pallas_call(
        functools.partial(kernel, sizes),
        out_shape=(out, out),
        in_specs=[pl.BlockSpec(memory_space=pltpu.HBM)] * 11,
        out_specs=(anywhere, anywhere),
        scratch_shapes=[
            pltpu.VMEM((2,) + flat, F32),
            pltpu.VMEM(upwind_pos.shape, F32),
            pltpu.VMEM(upwind_neg.shape, F32),
            pltpu.VMEM(collision.shape, F32),
            pltpu.VMEM(relax.shape, F32),
            pltpu.VMEM(wall_table.shape, F32),
            pltpu.VMEM(drag_weights.shape, F32),
            pltpu.VMEM(block_inverse.shape, F32),
            pltpu.VMEM(cell_codes.shape, jnp.int32),
            pltpu.VMEM(wall_mask.shape, jnp.int32),
            pltpu.VMEM((2, rows, padded, planes * width), F32),
            pltpu.VMEM((2, padded, width), F32),
            pltpu.VMEM((2, padded, width), F32),
            pltpu.VMEM((2, 2, padded, planes * width), F32),
            pltpu.VMEM((padded, BLOCKS * padded), F32),
            pltpu.VMEM((2, padded, BLOCKS * padded), BF16),
            pltpu.VMEM((2, padded, BLOCKS * padded), BF16),
            pltpu.VMEM((padded, 3 * padded), F32),
            pltpu.VMEM((2, 3, padded, 3 * padded), BF16),
            pltpu.VMEM((BLOCKS * padded, planes * width), BF16),
            pltpu.VMEM((BLOCKS * padded, planes * width), BF16),
            pltpu.VMEM((lowest * low_pad, 128), F32),
            pltpu.VMEM((lowest * low_pad, planes * width), F32),
            pltpu.VMEM((2, rows, low_pad, planes * width), F32),
            pltpu.VMEM((padded, planes * width), F32),
            pltpu.VMEM((8, padded), F32),
            pltpu.VMEM((2,) + flat, F32),
            pltpu.SemaphoreType.DMA((11,)),
            pltpu.SemaphoreType.DMA((2,)),
            pltpu.SemaphoreType.DMA((2,)),
            pltpu.SemaphoreType.DMA((2,)),
            pltpu.SemaphoreType.DMA((2, 2)),
            pltpu.SemaphoreType.DMA((2, 2)),
        ],
        compiler_params=pltpu.CompilerParams(
            collective_id=0, has_side_effects=True, vmem_limit_bytes=64 * 1024 * 1024
        ),
    )(
        state.reshape(flat), adjoint.reshape(flat), upwind_pos, upwind_neg, collision, relax,
        wall_table, drag_weights, block_inverse, cell_codes, wall_mask,
    )
    step = -(-flat[0] // (8 * PIECES)) * 8
    pieces = [(at, min(step, flat[0] - at)) for at in range(0, flat[0], step)]
    outs = pl.pallas_call(
        functools.partial(hand_over, pieces),
        out_shape=(out, out),
        in_specs=[anywhere] * 2,
        out_specs=(anywhere, anywhere),
        scratch_shapes=[
            pltpu.VMEM((2,) + flat, F32),
            pltpu.SemaphoreType.DMA((2, len(pieces))),
            pltpu.SemaphoreType.DMA((2, len(pieces))),
        ],
        compiler_params=pltpu.CompilerParams(vmem_limit_bytes=64 * 1024 * 1024),
    )(*outs)
    return tuple(o.reshape(state.shape) for o in outs)


def solution(mesh):
    in_specs = (
        P(None, None, "gy", "gx"),
        P(None, None, "gy", "gx"),
        P(),
        P(),
        P(),
        P(),
        P(),
        P(),
        P(),
        P(None, "gy", "gx"),
        P(None, "gy", "gx"),
    )
    out_specs = (P(None, None, "gy", "gx"), P(None, None, "gy", "gx"))
    return jax.shard_map(
        functools.partial(on_device, mesh.shape["gx"], mesh.shape["gy"]),
        mesh=mesh, in_specs=in_specs, out_specs=out_specs, check_vma=False,
    )
```
